32 devices in a mesh: row: 8 (over z, core), col: 4 (over y, x).
Axes of the slice: x: 2, y: 2, z: 4, core: 2. Of those that a mesh axis runs over, the one named last changes fastest.
Arguments:
- start_basis: float32 [32, 16384], P(None, ('row', 'col')), may hold values from -6 to 6
- degrees: float32 [16384], P(('row', 'col')), may hold values from 0.5 to 1.5
- tiles: float32 [1024, 256, 256], P(('row', 'col')), may hold values from -0.046875 to 0.046875
- tile_rows: int32 [8, 128], P('row', 'col'), may hold values from 0 to 7, as said below
- tile_cols: int32 [8, 128], P('row', 'col'), may hold values from 0 to 15
- counts: int32 [8, 4], P('row', 'col'), may hold values from 1 to 31, as said below
Outputs:
- basis: float32 [32, 16384], P(None, ('row', 'col'))
- projected: float32 [32, 32], replicated
The draws below stay inside these ranges and needn't reach their ends.
Inputs may be any that keep to these rules, and one draw needn't show every extreme that they name: `tile_rows`: the 32 (row, column) pairs of one device are distinct. counts[r, c] + counts[r', c] <= 32 where r' differs from r by 4; equality holds in column 0.
All inputs are finite; a program needn't handle non-finite values.
Results may differ from the reference program's by a relative error of at most 0.0003.
Values sent between devices are 32-bit elements; how exact they have to be, the bound alone decides.
No kernel may reach another device: no remote copies, remote signals or barrier semaphores. Data moves between devices by JAX's collectives and lax.ppermute only.
A program may use at most 64 MiB of HBM per device.

```python
import jax
import jax.numpy as jnp
from jax import lax

BS = 256
SUBSPACE = 32
BLK_DEV = 2
TMAX = 32
DEGREE = 3
NVERT = 16384
N_ROW = 8
N_COL = 4


def tile_grid(key):
    cells = N_COL * BLK_DEV * N_ROW * BLK_DEV

    def one_device(index):
        return jax.random.permutation(jax.random.fold_in(key, 1000 + index), cells)[:TMAX]
    picked = jax.vmap(one_device)(jnp.arange(N_ROW * N_COL, dtype=jnp.int32))
    return picked.reshape(N_ROW, N_COL * TMAX)


def draw_tile_rows(key, part):
    return (tile_grid(key) // (N_ROW * BLK_DEV)).astype(jnp.int32)


def draw_tile_cols(key, part):
    return (tile_grid(key) % (N_ROW * BLK_DEV)).astype(jnp.int32)


def draw_counts(key, part):
    pair_rows = N_ROW // 2
    heavy_first = jax.random.randint(jax.random.fold_in(key, 1), (pair_rows, N_COL), 0, 2)
    heavy_load = jax.random.randint(jax.random.fold_in(key, 2), (pair_rows, N_COL), 3 * TMAX // 4, TMAX)
    row_index = jnp.arange(pair_rows, dtype=jnp.int32)[:, None]
    column_index = jnp.arange(N_COL, dtype=jnp.int32)[None, :]
    corner = (row_index == 0) & (column_index == 0)
    heavy_load = jnp.where(corner, TMAX - 1, heavy_load)
    light_load = jax.random.randint(jax.random.fold_in(key, 3), (pair_rows, N_COL), 1, TMAX - heavy_load + 1)
    light_load = jnp.where(column_index == 0, TMAX - heavy_load, jnp.where(column_index == 1, 1, light_load))
    upper_half = jnp.where(heavy_first == 1, heavy_load, light_load)
    bottom = jnp.where(heavy_first == 1, light_load, heavy_load)
    return jnp.concatenate([upper_half, bottom], 0).astype(jnp.int32)


def block_scale(stream_key, shape, split, low, top_value):
    factor_of, own = 1.0, jax.random.fold_in(stream_key, 6)
    for dim, blocks in split:
        draws = jnp.exp(jax.random.uniform(jax.random.fold_in(own, dim), (blocks,), jnp.float32, low / len(split), top_value / len(split)))
        factor_of = factor_of * jnp.repeat(draws, shape[dim] // blocks).reshape([-1 if axis == dim else 1 for axis in range(len(shape))])
    return factor_of


def normal_values(stream_key, extent, spread, reach, split=(), held_as=jnp.bfloat16):
    array = spread * jax.random.normal(stream_key, extent, jnp.float32)
    if split:
        array = array * block_scale(stream_key, extent, split, -0.22, 0.18)
    return jnp.clip(array, -reach, reach).astype(held_as)


def setup_inputs(seed: int = 0) -> dict:
    splits = jax.random.split(jax.random.key(seed), 7)
    start_basis = normal_values(splits[0], (SUBSPACE, NVERT), 1.0, 6.0, ((1, 32),), jnp.float32)
    degrees = jnp.clip(0.5 + 1.0 * jax.random.uniform(splits[1], (NVERT,), jnp.float32) ** block_scale(splits[1], (NVERT,), ((0, 32),), -0.2, 0.2), 0.5, 1.5)
    tiles = normal_values(splits[2], (N_ROW * N_COL * TMAX, BS, BS), (4 * TMAX * BS // BLK_DEV) ** -0.5, 0.046875, ((0, 32),), jnp.float32)
    tile_rows = draw_tile_rows(jax.random.fold_in(splits[6], 71), 0)
    tile_cols = draw_tile_cols(jax.random.fold_in(splits[6], 71), 0)
    counts = draw_counts(jax.random.fold_in(splits[6], 71), 0)
    return {"start_basis": start_basis, "degrees": degrees, "tiles": tiles, "tile_rows": tile_rows, "tile_cols": tile_cols, "counts": counts}


center_shift = 1.0
spread_radius = 1.4
group_width = 8

def operator_apply(vectors, degrees, tiles, tile_rows, tile_cols, counts):
    block_total = N_ROW * N_COL * BLK_DEV
    blocks = vectors.reshape(SUBSPACE, block_total, BS)

    def per_device(total, device):
        row_index = device // N_COL
        col_index = device % N_COL
        own_tiles = lax.dynamic_slice_in_dim(tiles, device * TMAX, TMAX, 0)
        row_local = lax.dynamic_slice_in_dim(tile_rows[row_index], col_index * TMAX, TMAX, 0)
        col_local = lax.dynamic_slice_in_dim(tile_cols[row_index], col_index * TMAX, TMAX, 0)
        row_global = ((row_index * N_COL + row_local // BLK_DEV) * BLK_DEV + row_local % BLK_DEV).astype(jnp.int32)
        col_global = ((col_local // BLK_DEV * N_COL + col_index) * BLK_DEV + col_local % BLK_DEV).astype(jnp.int32)
        live = counts[row_index, col_index]

        def add_group(index, inner):
            start = (index * group_width).astype(jnp.int32)
            group_tiles = lax.dynamic_slice_in_dim(own_tiles, start, group_width, 0)
            group_rows = lax.dynamic_slice_in_dim(row_global, start, group_width, 0)
            group_cols = lax.dynamic_slice_in_dim(col_global, start, group_width, 0)
            picked = jnp.take(blocks, group_cols, axis=1)
            product = jnp.einsum('kgj,gij->kgi', picked, group_tiles, precision=lax.Precision.HIGHEST)
            valid = (start + jnp.arange(group_width, dtype=jnp.int32) < live).astype(jnp.float32)
            return inner.at[:, group_rows, :].add(product * valid[None, :, None])
        total = lax.fori_loop(0, (live + group_width - 1) // group_width, add_group, total)
        return (total, None)
    initial = jnp.zeros((SUBSPACE, block_total, BS), jnp.float32)
    total, unused = lax.scan(per_device, initial, jnp.arange(N_ROW * N_COL, dtype=jnp.int32))
    return degrees[None, :] * vectors - total.reshape(SUBSPACE, block_total * BS)

def reference(start_basis, degrees, tiles, tile_rows, tile_cols, counts):
    nverts = N_ROW * N_COL * BLK_DEV * BS

    def shifted(vectors):
        image = operator_apply(vectors, degrees, tiles, tile_rows, tile_cols, counts)
        return (image - center_shift * vectors) / spread_radius
    previous = start_basis
    current = shifted(start_basis)
    for level in range(DEGREE - 1):
        following = 2.0 * shifted(current) - previous
        previous, current = (current, following)
    gram_matrix = jnp.einsum('kn,mn->km', current, current, precision=lax.Precision.HIGHEST) / nverts
    factor = jnp.linalg.cholesky(gram_matrix)
    basis = jax.scipy.linalg.solve_triangular(factor, current, lower=True)
    image = operator_apply(basis, degrees, tiles, tile_rows, tile_cols, counts)
    moment = jnp.einsum('kn,mn->km', basis, image, precision=lax.Precision.HIGHEST) / nverts
    projected = 0.5 * (moment + moment.T)
    return (basis, projected)
```

```python
import functools

import jax
import jax.numpy as jnp
from jax import lax
from jax.experimental import pallas as pl
from jax.experimental.pallas import tpu as pltpu
from jax.sharding import PartitionSpec as P

DEGREE = 3


center_shift = 1.0
spread_radius = 1.4
MIB = 1 << 20

ROWS_BY_ROWS = (((1,), (1,)), ((), ()))


def dot_rows(left, right, precision=None):
    return lax.dot_general(
        left, right, ROWS_BY_ROWS, precision=precision, preferred_element_type=jnp.float32
    )


def split(value):
    high = value.astype(jnp.bfloat16)
    low = (value - high.astype(jnp.float32)).astype(jnp.bfloat16)
    return high, low


def accumulate_tiles(slots, tiles, parts, halves, total):
    subspace = parts[0].shape[0]
    edge = tiles.shape[1]
    per_part = parts[0].shape[1] // edge
    for index, part in enumerate(parts):
        for block in range(per_part):
            high, low = split(part[:, block * edge : (block + 1) * edge])
            halves[index * per_part + block, :subspace] = high
            halves[index * per_part + block, subspace:] = low
    total[...] = jnp.zeros_like(total)
    for slot in range(tiles.shape[0]):
        vectors = halves[slots[1, slot]]
        tile_high, tile_low = split(tiles[slot])
        first = dot_rows(vectors, tile_high)
        second = dot_rows(vectors[:subspace], tile_low)
        total[slots[0, slot]] += first[:subspace] + first[subspace:] + second


def product_kernel(n_row, n_col, slots, tiles, *refs):
    parts, outs = refs[:n_row], refs[n_row : n_row + n_col]
    halves, total = refs[n_row + n_col :]
    accumulate_tiles(slots, tiles, parts, halves, total)
    edge = tiles.shape[1]
    per_part = parts[0].shape[1] // edge
    for index, out in enumerate(outs):
        for block in range(per_part):
            out[:, block * edge : (block + 1) * edge] = total[index * per_part + block]


def moment_kernel(n_row, n_col, slots, tiles, degrees, *refs):
    parts, sides = refs[:n_row], refs[n_row : n_row + n_col - 1]
    out, halves, total = refs[n_row + n_col - 1 :]
    accumulate_tiles(slots, tiles, parts, halves, total)
    edge = tiles.shape[1]
    subspace, width = parts[0].shape
    per_part = width // edge
    own = parts[0][...]
    gram = dot_rows(own, own, lax.Precision.HIGHEST)
    moment = dot_rows(own, own * degrees[...], lax.Precision.HIGHEST)
    for index, side in enumerate((parts[0], *sides)):
        for block in range(per_part):
            left = jnp.concatenate(split(side[:, block * edge : (block + 1) * edge]), 0)
            right = jnp.concatenate(split(total[index * per_part + block]), 0)
            both = dot_rows(left, right)
            both = both[:subspace] + both[subspace:]
            moment -= both[:, :subspace] + both[:, subspace:]
    out[...] = jnp.concatenate([gram, moment], 1)


def finish_kernel(nverts, sums, filtered, basis, projected):
    subspace = filtered.shape[0]
    both = sums[...] * (1.0 / nverts)
    gram, moment = both[:, :subspace], both[:, subspace:]
    row = lax.broadcasted_iota(jnp.int32, (subspace, subspace), 0)
    column = lax.broadcasted_iota(jnp.int32, (subspace, subspace), 1)
    work = jnp.concatenate([gram, (row == column).astype(jnp.float32)], 1)
    wide_row = lax.broadcasted_iota(jnp.int32, (subspace, 2 * subspace), 0)
    scale = jnp.zeros((subspace, 1), jnp.float32)
    for step in range(subspace):
        pivot = work[step : step + 1, step : step + 1]
        scale = jnp.where(wide_row[:, :1] == step, lax.rsqrt(pivot), scale)
        ratio = work[:, step : step + 1] / pivot
        work = jnp.where(wide_row > step, work - ratio * work[step : step + 1, :], work)
    inverse = scale * work[:, subspace:]
    highest = lax.Precision.HIGHEST
    basis[...] = jnp.dot(
        inverse, filtered[...], precision=highest, preferred_element_type=jnp.float32
    )
    half = jnp.dot(inverse, moment, precision=highest, preferred_element_type=jnp.float32)
    whole = dot_rows(half, inverse, highest)
    projected[...] = 0.5 * (whole + whole.T)


def body(n_row, n_col, start_basis, degrees, tiles, tile_rows, tile_cols, counts):
    subspace, width = start_basis.shape
    slots_held, edge = tiles.shape[0], tiles.shape[1]
    per_part = width // edge
    nverts = n_row * n_col * width
    row, col = lax.axis_index("row"), lax.axis_index("col")
    degrees = degrees[None, :]

    row_local, col_local = tile_rows[0], tile_cols[0]
    row_place = ((row_local // per_part) ^ col) * per_part + row_local % per_part
    col_place = ((col_local // per_part) ^ row) * per_part + col_local % per_part
    live = jnp.arange(slots_held, dtype=jnp.int32) < counts[0, 0]
    spare = n_col * per_part
    slots = jnp.stack([jnp.where(live, row_place, spare), col_place])

    def swap(value, axis, size, distance):
        return lax.ppermute(value, axis, [(i, i ^ distance) for i in range(size)])

    def gather_row(value):
        parts = [None] * n_row
        parts[0] = value
        for distance in range(2, n_row, 2):
            parts[distance] = swap(value, "row", n_row, distance)
        for distance in range(0, n_row, 2):
            parts[distance + 1] = swap(parts[distance], "row", n_row, 1)
        return parts

    def gather_col(value):
        return [swap(value, "col", n_col, distance) for distance in range(1, n_col)]

    def vmem(count):
        return [pl.BlockSpec(memory_space=pltpu.VMEM)] * count

    scratch = [
        pltpu.VMEM((n_row * per_part, 2 * subspace, edge), jnp.bfloat16),
        pltpu.VMEM((n_col * per_part + 1, subspace, edge), jnp.float32),
    ]
    slots_spec = pl.BlockSpec(memory_space=pltpu.SMEM)
    params = pltpu.CompilerParams(vmem_limit_bytes=20 * MIB)
    piece = jax.ShapeDtypeStruct((subspace, width), jnp.float32)

    def weights(vectors):
        partial_values = pl.pallas_call(
            functools.partial(product_kernel, n_row, n_col),
            out_shape=[piece] * n_col,
            in_specs=[slots_spec, *vmem(1 + n_row)],
            out_specs=vmem(n_col),
            scratch_shapes=scratch,
            compiler_params=params,
            name="tile_products",
        )(slots, tiles, *gather_row(vectors))
        total = partial_values[0]
        for distance in range(1, n_col):
            total = total + swap(partial_values[distance], "col", n_col, distance)
        return total

    def shifted(vectors):
        return ((degrees - center_shift) * vectors - weights(vectors)) / spread_radius

    previous = start_basis
    filtered = shifted(start_basis)
    for level in range(DEGREE - 1):
        following = 2.0 * shifted(filtered) - previous
        previous, filtered = (filtered, following)

    sums = pl.pallas_call(
        functools.partial(moment_kernel, n_row, n_col),
        out_shape=jax.ShapeDtypeStruct((subspace, 2 * subspace), jnp.float32),
        in_specs=[slots_spec, *vmem(2 + n_row + n_col - 1)],
        out_specs=pl.BlockSpec(memory_space=pltpu.VMEM),
        scratch_shapes=scratch,
        compiler_params=params,
        name="moment",
    )(slots, tiles, degrees, *gather_row(filtered), *gather_col(filtered))
    sums = sums + swap(sums, "row", n_row, 1)
    sums = sum([swap(sums, "row", n_row, distance) for distance in range(2, n_row, 2)], sums)
    sums = sum([swap(sums, "col", n_col, distance) for distance in range(1, n_col)], sums)
    basis, projected = pl.pallas_call(
        functools.partial(finish_kernel, nverts),
        out_shape=[piece, jax.ShapeDtypeStruct((subspace, subspace), jnp.float32)],
        in_specs=vmem(2),
        out_specs=vmem(2),
        compiler_params=params,
        name="finish",
    )(sums, filtered)
    return (basis, projected)


def solution(mesh):
    return jax.shard_map(
        functools.partial(body, mesh.shape["row"], mesh.shape["col"]),
        mesh=mesh,
        in_specs=(
            P(None, ("row", "col")),
            P(("row", "col")),
            P(("row", "col"), None, None),
            P("row", "col"),
            P("row", "col"),
            P("row", "col"),
        ),
        out_specs=(P(None, ("row", "col")), P()),
        check_vma=False,
    )
```

```python
import functools

import jax
import jax.numpy as jnp
from jax import lax
from jax.experimental import pallas as pl
from jax.experimental.pallas import tpu as pltpu
from jax.sharding import PartitionSpec as P

DEGREE = 3


center_shift = 1.0
spread_radius = 1.4
MIB = 1 << 20

ROWS_BY_ROWS = (((1,), (1,)), ((), ()))


def dot_rows(left, right, precision=None):
    return lax.dot_general(
        left, right, ROWS_BY_ROWS, precision=precision, preferred_element_type=jnp.float32
    )


def split(value):
    high = value.astype(jnp.bfloat16)
    low = (value - high.astype(jnp.float32)).astype(jnp.bfloat16)
    return high, low


def stage_kernel(tiles, high, low, arrived, sems):
    chunks = sems.shape[0]
    width = tiles.shape[0] // chunks
    copies = [
        pltpu.make_async_copy(
            tiles.at[pl.ds(chunk * width, width)], arrived.at[pl.ds(chunk * width, width)], sems.at[chunk]
        )
        for chunk in range(chunks)
    ]
    for copy in copies:
        copy.start()
    for chunk, copy in enumerate(copies):
        copy.wait()
        for slot in range(chunk * width, (chunk + 1) * width):
            high[slot], low[slot] = split(arrived[slot].T)


def accumulate_tiles(slots, high, low, parts, halves, total):
    subspace = parts[0].shape[0]
    edge = high.shape[1]
    per_part = parts[0].shape[1] // edge
    places = slots[...]
    for index, part in enumerate(parts):
        for block in range(per_part):
            upper, lower = split(part[:, block * edge : (block + 1) * edge])
            halves[index * per_part + block, :subspace] = upper
            halves[index * per_part + block, subspace:] = lower
    total[...] = jnp.zeros_like(total)
    for slot in range(high.shape[0]):
        vectors = halves[places[1, slot]]
        first = jnp.dot(vectors, high[slot], preferred_element_type=jnp.float32)
        second = jnp.dot(vectors[:subspace], low[slot], preferred_element_type=jnp.float32)
        total[places[0, slot]] += first[:subspace] + first[subspace:] + second


def product_kernel(n_row, n_col, slots, high, low, *refs):
    parts, outs = refs[:n_row], refs[n_row : n_row + n_col]
    halves, total = refs[n_row + n_col :]
    accumulate_tiles(slots, high, low, parts, halves, total)
    edge = high.shape[1]
    per_part = parts[0].shape[1] // edge
    for index, out in enumerate(outs):
        for block in range(per_part):
            out[:, block * edge : (block + 1) * edge] = total[index * per_part + block]


def moment_kernel(n_row, n_col, slots, high, low, degrees, *refs):
    parts, sides = refs[:n_row], refs[n_row : n_row + n_col - 1]
    out, halves, total = refs[n_row + n_col - 1 :]
    accumulate_tiles(slots, high, low, parts, halves, total)
    edge = high.shape[1]
    subspace, width = parts[0].shape
    per_part = width // edge
    own = parts[0][...]
    gram = dot_rows(own, own, lax.Precision.HIGHEST)
    moment = dot_rows(own, own * degrees[...], lax.Precision.HIGHEST)
    for index, side in enumerate((parts[0], *sides)):
        for block in range(per_part):
            left = jnp.concatenate(split(side[:, block * edge : (block + 1) * edge]), 0)
            right = jnp.concatenate(split(total[index * per_part + block]), 0)
            both = dot_rows(left, right)
            both = both[:subspace] + both[subspace:]
            moment -= both[:, :subspace] + both[:, subspace:]
    out[...] = jnp.concatenate([gram, moment], 1)


def eliminate(work, size, panel):
    row = lax.broadcasted_iota(jnp.int32, work.shape, 0)
    pivots = jnp.ones_like(work)
    for first in range(0, size, panel):
        columns = [
            jnp.broadcast_to(work[:, index : index + 1], work.shape)
            for index in range(first, first + panel)
        ]
        for index in range(panel):
            step = first + index
            pivot = columns[index][step : step + 1, :]
            pivots = jnp.where(row == step, pivot, pivots)
            ratio = jnp.where(row > step, columns[index], 0.0) * (1.0 / pivot)
            work = work - ratio * work[step : step + 1, :]
            for later in range(index + 1, panel):
                columns[later] = columns[later] - ratio * columns[later][step : step + 1, :]
    return work, lax.rsqrt(pivots)


def finish_kernel(nverts, sums, filtered, basis, projected):
    subspace = filtered.shape[0]
    both = sums[...] * (1.0 / nverts)
    gram, moment = both[:, :subspace], both[:, subspace:]
    moment = 0.5 * (moment + moment.T)
    row = lax.broadcasted_iota(jnp.int32, (subspace, subspace), 0)
    column = lax.broadcasted_iota(jnp.int32, (subspace, subspace), 1)
    identity = (row == column).astype(jnp.float32)
    work, scale = eliminate(jnp.concatenate([gram, identity, moment], 1), subspace, 8)
    work = work * scale
    inverse, half = work[:, subspace : 2 * subspace], work[:, 2 * subspace :]
    projected[...] = dot_rows(half, inverse, lax.Precision.HIGHEST)
    basis[...] = jnp.dot(
        inverse, filtered[...], precision=lax.Precision.HIGHEST, preferred_element_type=jnp.float32
    )


def body(n_row, n_col, start_basis, degrees, tiles, tile_rows, tile_cols, counts):
    subspace, width = start_basis.shape
    slots_held, edge = tiles.shape[0], tiles.shape[1]
    per_part = width // edge
    nverts = n_row * n_col * width
    row, col = lax.axis_index("row"), lax.axis_index("col")
    degrees = degrees[None, :]

    row_local, col_local = tile_rows[0], tile_cols[0]
    row_place = ((row_local // per_part) ^ col) * per_part + row_local % per_part
    col_place = ((col_local // per_part) ^ row) * per_part + col_local % per_part
    live = jnp.arange(slots_held, dtype=jnp.int32) < counts[0, 0]
    spare = n_col * per_part
    slots = jnp.stack([jnp.where(live, row_place, spare), col_place])

    def swap(value, axis, size, distance):
        return lax.ppermute(value, axis, [(i, i ^ distance) for i in range(size)])

    def gather_row(value):
        parts = [None] * n_row
        parts[0] = value
        for distance in range(2, n_row, 2):
            parts[distance] = swap(value, "row", n_row, distance)
        for distance in range(0, n_row, 2):
            parts[distance + 1] = swap(parts[distance], "row", n_row, 1)
        return parts

    def gather_col(value):
        return [swap(value, "col", n_col, distance) for distance in range(1, n_col)]

    def vmem(count):
        return [pl.BlockSpec(memory_space=pltpu.VMEM)] * count

    scratch = [
        pltpu.VMEM((n_row * per_part, 2 * subspace, edge), jnp.bfloat16),
        pltpu.VMEM((n_col * per_part + 1, subspace, edge), jnp.float32),
    ]
    params = pltpu.CompilerParams(vmem_limit_bytes=20 * MIB)
    piece = jax.ShapeDtypeStruct((subspace, width), jnp.float32)
    high, low = pl.pallas_call(
        stage_kernel,
        out_shape=[jax.ShapeDtypeStruct(tiles.shape, jnp.bfloat16)] * 2,
        in_specs=[pl.BlockSpec(memory_space=pltpu.HBM)],
        out_specs=vmem(2),
        scratch_shapes=[
            pltpu.VMEM(tiles.shape, jnp.float32),
            pltpu.SemaphoreType.DMA((slots_held // 2,)),
        ],
        compiler_params=pltpu.CompilerParams(vmem_limit_bytes=42 * MIB),
        name="stage",
    )(tiles)

    def weights(vectors):
        partial_values = pl.pallas_call(
            functools.partial(product_kernel, n_row, n_col),
            out_shape=[piece] * n_col,
            in_specs=vmem(3 + n_row),
            out_specs=vmem(n_col),
            scratch_shapes=scratch,
            compiler_params=params,
            name="tile_products",
        )(slots, high, low, *gather_row(vectors))
        total = partial_values[0]
        for distance in range(1, n_col):
            total = total + swap(partial_values[distance], "col", n_col, distance)
        return total

    def shifted(vectors):
        return ((degrees - center_shift) * vectors - weights(vectors)) / spread_radius

    previous = start_basis
    filtered = shifted(start_basis)
    for level in range(DEGREE - 1):
        following = 2.0 * shifted(filtered) - previous
        previous, filtered = (filtered, following)

    sums = pl.pallas_call(
        functools.partial(moment_kernel, n_row, n_col),
        out_shape=jax.ShapeDtypeStruct((subspace, 2 * subspace), jnp.float32),
        in_specs=vmem(4 + n_row + n_col - 1),
        out_specs=pl.BlockSpec(memory_space=pltpu.VMEM),
        scratch_shapes=scratch,
        compiler_params=params,
        name="moment",
    )(slots, high, low, degrees, *gather_row(filtered), *gather_col(filtered))
    sums = sums + swap(sums, "row", n_row, 1)
    sums = sum([swap(sums, "row", n_row, distance) for distance in range(2, n_row, 2)], sums)
    sums = sum([swap(sums, "col", n_col, distance) for distance in range(1, n_col)], sums)
    basis, projected = pl.pallas_call(
        functools.partial(finish_kernel, nverts),
        out_shape=[piece, jax.ShapeDtypeStruct((subspace, subspace), jnp.float32)],
        in_specs=vmem(2),
        out_specs=vmem(2),
        compiler_params=params,
        name="finish",
    )(sums, filtered)
    return (basis, projected)


def solution(mesh):
    return jax.shard_map(
        functools.partial(body, mesh.shape["row"], mesh.shape["col"]),
        mesh=mesh,
        in_specs=(
            P(None, ("row", "col")),
            P(("row", "col")),
            P(("row", "col"), None, None),
            P("row", "col"),
            P("row", "col"),
            P("row", "col"),
        ),
        out_specs=(P(None, ("row", "col")), P()),
        check_vma=False,
    )
```

```python
import functools

import jax
import jax.numpy as jnp
from jax import lax
from jax.experimental import pallas as pl
from jax.experimental.pallas import tpu as pltpu
from jax.sharding import PartitionSpec as P

DEGREE = 3


center_shift = 1.0
spread_radius = 1.4
MIB = 1 << 20

ROWS_BY_ROWS = (((1,), (1,)), ((), ()))


def dot_rows(left, right, precision=None):
    return lax.dot_general(
        left, right, ROWS_BY_ROWS, precision=precision, preferred_element_type=jnp.float32
    )


def split(value):
    high = value.astype(jnp.bfloat16)
    low = (value - high.astype(jnp.float32)).astype(jnp.bfloat16)
    return high, low


def place_slots(n_col, per_part, rows, columns, counts):
    shift = per_part.bit_length() - 1
    row = rows[...] ^ (lax.axis_index("col") << shift)
    column = columns[...] ^ (lax.axis_index("row") << shift)
    live = lax.broadcasted_iota(jnp.int32, row.shape, 1) < counts[...]
    return jnp.concatenate([jnp.where(live, row, n_col * per_part), column], 0)


def place_kernel(n_col, per_part, rows, columns, counts, places):
    places[...] = place_slots(n_col, per_part, rows, columns, counts)


def stage_kernel(tiles, high, low, arrived, sems):
    chunks = sems.shape[0]
    width = tiles.shape[0] // chunks
    copies = [
        pltpu.make_async_copy(
            tiles.at[pl.ds(chunk * width, width)], arrived.at[pl.ds(chunk * width, width)], sems.at[chunk]
        )
        for chunk in range(chunks)
    ]
    for copy in copies:
        copy.start()
    for chunk, copy in enumerate(copies):
        copy.wait()
        for slot in range(chunk * width, (chunk + 1) * width):
            high[slot], low[slot] = split(arrived[slot].T)


def accumulate_tiles(slots, high, low, parts, halves, total):
    subspace = parts[0].shape[0]
    edge = high.shape[1]
    per_part = parts[0].shape[1] // edge
    places = slots[...]
    for index, part in enumerate(parts):
        for block in range(per_part):
            upper, lower = split(part[:, block * edge : (block + 1) * edge])
            halves[index * per_part + block, :subspace] = upper
            halves[index * per_part + block, subspace:] = lower
    total[...] = jnp.zeros_like(total)
    for slot in range(high.shape[0]):
        vectors = halves[places[1, slot]]
        first = jnp.dot(vectors, high[slot], preferred_element_type=jnp.float32)
        second = jnp.dot(vectors[:subspace], low[slot], preferred_element_type=jnp.float32)
        total[places[0, slot]] += first[:subspace] + first[subspace:] + second


def product_kernel(n_row, n_col, slots, high, low, *refs):
    parts, outs = refs[:n_row], refs[n_row : n_row + n_col]
    halves, total = refs[n_row + n_col :]
    accumulate_tiles(slots, high, low, parts, halves, total)
    edge = high.shape[1]
    per_part = parts[0].shape[1] // edge
    for index, out in enumerate(outs):
        for block in range(per_part):
            out[:, block * edge : (block + 1) * edge] = total[index * per_part + block]


def moment_kernel(n_row, n_col, degrees, *refs):
    parts, sides, products = refs[:n_row], refs[n_row : n_row + n_col - 1], refs[n_row + n_col - 1 : -1]
    out = refs[-1]
    subspace = parts[0].shape[0]

    def quarters(left, right):
        both = dot_rows(left, right)
        both = both[:subspace] + both[subspace:]
        return both[:, :subspace] + both[:, subspace:]

    own = parts[0][...]
    moment = dot_rows(own, own * degrees[...], lax.Precision.HIGHEST)
    gram = jnp.zeros_like(moment)
    for part in parts:
        both = jnp.concatenate(split(part[...]), 0)
        gram += quarters(both, both)
    for side, product in zip((parts[0], *sides), products):
        moment -= quarters(
            jnp.concatenate(split(side[...]), 0), jnp.concatenate(split(product[...]), 0)
        )
    out[...] = jnp.concatenate([gram, moment], 1)


def eliminate(work, size, panel):
    row = lax.broadcasted_iota(jnp.int32, work.shape, 0)
    pivots = jnp.ones_like(work)
    for first in range(0, size, panel):
        columns = [
            jnp.broadcast_to(work[:, index : index + 1], work.shape)
            for index in range(first, first + panel)
        ]
        for index in range(panel):
            step = first + index
            pivot = columns[index][step : step + 1, :]
            pivots = jnp.where(row == step, pivot, pivots)
            ratio = jnp.where(row > step, columns[index], 0.0) * (1.0 / pivot)
            work = work - ratio * work[step : step + 1, :]
            for later in range(index + 1, panel):
                columns[later] = columns[later] - ratio * columns[later][step : step + 1, :]
    return work, lax.rsqrt(pivots)


def factor_kernel(nverts, sums, filtered, inverse, basis):
    subspace = filtered.shape[0]
    gram = sums[:, :subspace] * (1.0 / nverts)
    row = lax.broadcasted_iota(jnp.int32, (subspace, subspace), 0)
    column = lax.broadcasted_iota(jnp.int32, (subspace, subspace), 1)
    identity = (row == column).astype(jnp.float32)
    work, scale = eliminate(jnp.concatenate([gram, identity], 1), subspace, 8)
    solved = (work * scale)[:, subspace:]
    inverse[...] = solved
    basis[...] = jnp.dot(
        solved, filtered[...], precision=lax.Precision.HIGHEST, preferred_element_type=jnp.float32
    )


def project_kernel(nverts, sums, inverse, projected):
    subspace = inverse.shape[0]
    moment = sums[:, subspace:] * (0.5 / nverts)
    half = jnp.dot(
        inverse[...],
        moment + moment.T,
        precision=lax.Precision.HIGHEST,
        preferred_element_type=jnp.float32,
    )
    projected[...] = dot_rows(half, inverse[...], lax.Precision.HIGHEST)


def body(n_row, n_col, start_basis, degrees, tiles, tile_rows, tile_cols, counts):
    subspace, width = start_basis.shape
    slots_held, edge = tiles.shape[0], tiles.shape[1]
    per_part = width // edge
    nverts = n_row * n_col * width
    degrees = degrees[None, :]

    def swap(value, axis, size, distance):
        return lax.ppermute(value, axis, [(i, i ^ distance) for i in range(size)])

    def gather_row(value, behind=None):
        parts = [None] * n_row
        parts[0] = value
        for distance in range(2, n_row, 2):
            parts[distance] = swap(value, "row", n_row, distance)
        if behind is not None:
            parts[2::2], behind = lax.optimization_barrier((parts[2::2], behind))
        for distance in range(0, n_row, 2):
            parts[distance + 1] = swap(parts[distance], "row", n_row, 1)
        return parts if behind is None else (parts, behind)

    def gather_col(value):
        return [swap(value, "col", n_col, distance) for distance in range(1, n_col)]

    def vmem(count):
        return [pl.BlockSpec(memory_space=pltpu.VMEM)] * count

    scratch = [
        pltpu.VMEM((n_row * per_part, 2 * subspace, edge), jnp.bfloat16),
        pltpu.VMEM((n_col * per_part + 1, subspace, edge), jnp.float32),
    ]
    params = pltpu.CompilerParams(vmem_limit_bytes=20 * MIB)
    piece = jax.ShapeDtypeStruct((subspace, width), jnp.float32)
    slots = pl.pallas_call(
        functools.partial(place_kernel, n_col, per_part),
        out_shape=jax.ShapeDtypeStruct((2, slots_held), jnp.int32),
        in_specs=vmem(3),
        out_specs=pl.BlockSpec(memory_space=pltpu.VMEM),
        compiler_params=params,
        name="places",
    )(tile_rows, tile_cols, counts)
    high, low = pl.pallas_call(
        stage_kernel,
        out_shape=[jax.ShapeDtypeStruct(tiles.shape, jnp.bfloat16)] * 2,
        in_specs=[pl.BlockSpec(memory_space=pltpu.HBM)],
        out_specs=vmem(2),
        scratch_shapes=[
            pltpu.VMEM(tiles.shape, jnp.float32),
            pltpu.SemaphoreType.DMA((slots_held // 2,)),
        ],
        compiler_params=pltpu.CompilerParams(vmem_limit_bytes=42 * MIB),
        name="stage",
    )(tiles)

    parts, (slots, high, low) = gather_row(start_basis, (slots, high, low))

    def products(parts):
        return pl.pallas_call(
            functools.partial(product_kernel, n_row, n_col),
            out_shape=[piece] * n_col,
            in_specs=vmem(3 + n_row),
            out_specs=vmem(n_col),
            scratch_shapes=scratch,
            compiler_params=params,
            name="tile_products",
        )(slots, high, low, *parts)

    def weights(parts):
        partial_values = products(parts)
        total = partial_values[0]
        for distance in reversed(range(1, n_col)):
            total = total + swap(partial_values[distance], "col", n_col, distance)
        return total

    def shifted(vectors, parts=None):
        parts = gather_row(vectors) if parts is None else parts
        return ((degrees - center_shift) * vectors - weights(parts)) / spread_radius

    previous = start_basis
    filtered = shifted(start_basis, parts)
    for level in range(DEGREE - 1):
        following = 2.0 * shifted(filtered) - previous
        previous, filtered = (filtered, following)

    parts = gather_row(filtered)
    beside = filtered
    sides = gather_col(beside)
    sides, parts[n_row // 2 + 1] = lax.optimization_barrier((sides, parts[n_row // 2 + 1]))
    pieces = products(parts)
    sums = pl.pallas_call(
        functools.partial(moment_kernel, n_row, n_col),
        out_shape=jax.ShapeDtypeStruct((subspace, 2 * subspace), jnp.float32),
        in_specs=vmem(n_row + 2 * n_col),
        out_specs=pl.BlockSpec(memory_space=pltpu.VMEM),
        compiler_params=params,
        name="moment",
    )(degrees, *parts, *sides, *pieces)
    sums = sum([swap(sums, "col", n_col, distance) for distance in range(1, n_col)], sums)
    inverse, basis = pl.pallas_call(
        functools.partial(factor_kernel, nverts),
        out_shape=[jax.ShapeDtypeStruct((subspace, subspace), jnp.float32), piece],
        in_specs=vmem(2),
        out_specs=vmem(2),
        compiler_params=params,
        name="factor",
    )(sums, filtered)
    arrived = [swap(sums, "row", n_row, distance) for distance in range(2, n_row, 2)]
    arrived, inverse = lax.optimization_barrier((arrived, inverse))
    sums = sum(arrived, sums)
    sums = sums + swap(sums, "row", n_row, 1)
    projected = pl.pallas_call(
        functools.partial(project_kernel, nverts),
        out_shape=jax.ShapeDtypeStruct((subspace, subspace), jnp.float32),
        in_specs=vmem(2),
        out_specs=pl.BlockSpec(memory_space=pltpu.VMEM),
        compiler_params=params,
        name="project",
    )(sums, inverse)
    return (basis, projected)


def solution(mesh):
    return jax.shard_map(
        functools.partial(body, mesh.shape["row"], mesh.shape["col"]),
        mesh=mesh,
        in_specs=(
            P(None, ("row", "col")),
            P(("row", "col")),
            P(("row", "col"), None, None),
            P("row", "col"),
            P("row", "col"),
            P("row", "col"),
        ),
        out_specs=(P(None, ("row", "col")), P()),
        check_vma=False,
    )
```

```python
import functools

import jax
import jax.numpy as jnp
from jax import lax
from jax.experimental import pallas as pl
from jax.experimental.pallas import tpu as pltpu
from jax.sharding import PartitionSpec as P

DEGREE = 3


center_shift = 1.0
spread_radius = 1.4
MIB = 1 << 20

ROWS_BY_ROWS = (((1,), (1,)), ((), ()))


def dot_rows(left, right, precision=None):
    return lax.dot_general(
        left, right, ROWS_BY_ROWS, precision=precision, preferred_element_type=jnp.float32
    )


def split(value):
    high = value.astype(jnp.bfloat16)
    low = (value - high.astype(jnp.float32)).astype(jnp.bfloat16)
    return high, low


def place_slots(n_col, per_part, rows, columns, counts):
    shift = per_part.bit_length() - 1
    row = rows[...] ^ (lax.axis_index("col") << shift)
    column = columns[...] ^ (lax.axis_index("row") << shift)
    live = lax.broadcasted_iota(jnp.int32, row.shape, 1) < counts[...]
    return jnp.concatenate([jnp.where(live, row, n_col * per_part), column], 0)


def place_kernel(n_col, per_part, rows, columns, counts, places):
    places[...] = place_slots(n_col, per_part, rows, columns, counts)


def stage_kernel(tiles, high, low, arrived, sems):
    chunks = sems.shape[0]
    width = tiles.shape[0] // chunks
    copies = [
        pltpu.make_async_copy(
            tiles.at[pl.ds(chunk * width, width)], arrived.at[pl.ds(chunk * width, width)], sems.at[chunk]
        )
        for chunk in range(chunks)
    ]
    for copy in copies:
        copy.start()
    for chunk, copy in enumerate(copies):
        copy.wait()
        for slot in range(chunk * width, (chunk + 1) * width):
            high[slot], low[slot] = split(arrived[slot].T)


def accumulate_tiles(slots, high, low, parts, halves, total):
    subspace = parts[0].shape[0]
    edge = high.shape[1]
    per_part = parts[0].shape[1] // edge
    places = slots[...]
    for index, part in enumerate(parts):
        for block in range(per_part):
            upper, lower = split(part[:, block * edge : (block + 1) * edge])
            halves[index * per_part + block, :subspace] = upper
            halves[index * per_part + block, subspace:] = lower
    total[...] = jnp.zeros_like(total)
    for slot in range(high.shape[0]):
        vectors = halves[places[1, slot]]
        first = jnp.dot(vectors, high[slot], preferred_element_type=jnp.float32)
        second = jnp.dot(vectors[:subspace], low[slot], preferred_element_type=jnp.float32)
        total[places[0, slot]] += first[:subspace] + first[subspace:] + second


def product_kernel(n_row, n_col, slots, high, low, *refs):
    parts, outs = refs[:n_row], refs[n_row : n_row + n_col]
    halves, total = refs[n_row + n_col :]
    accumulate_tiles(slots, high, low, parts, halves, total)
    edge = high.shape[1]
    per_part = parts[0].shape[1] // edge
    for index, out in enumerate(outs):
        for block in range(per_part):
            out[:, block * edge : (block + 1) * edge] = total[index * per_part + block]


def moment_kernel(n_row, n_col, degrees, *refs):
    parts, sides, products = refs[:n_row], refs[n_row : n_row + n_col - 1], refs[n_row + n_col - 1 : -1]
    out = refs[-1]
    subspace = parts[0].shape[0]

    def quarters(left, right):
        both = dot_rows(left, right)
        both = both[:subspace] + both[subspace:]
        return both[:, :subspace] + both[:, subspace:]

    own = parts[0][...]
    moment = dot_rows(own, own * degrees[...], lax.Precision.HIGHEST)
    gram = jnp.zeros_like(moment)
    for part in parts:
        both = jnp.concatenate(split(part[...]), 0)
        gram += quarters(both, both)
    for side, product in zip((parts[0], *sides), products):
        moment -= quarters(
            jnp.concatenate(split(side[...]), 0), jnp.concatenate(split(product[...]), 0)
        )
    out[...] = jnp.concatenate([gram, moment], 1)


def eliminate(work, size, panel):
    row = lax.broadcasted_iota(jnp.int32, work.shape, 0)
    pivots = jnp.ones_like(work)
    for first in range(0, size, panel):
        columns = [
            jnp.broadcast_to(work[:, index : index + 1], work.shape)
            for index in range(first, first + panel)
        ]
        for index in range(panel):
            step = first + index
            pivot = columns[index][step : step + 1, :]
            pivots = jnp.where(row == step, pivot, pivots)
            ratio = jnp.where(row > step, columns[index], 0.0) * (1.0 / pivot)
            work = work - ratio * work[step : step + 1, :]
            for later in range(index + 1, panel):
                columns[later] = columns[later] - ratio * columns[later][step : step + 1, :]
    return work, lax.rsqrt(pivots)


def factor_kernel(nverts, sums, filtered, inverse, basis):
    subspace = filtered.shape[0]
    gram = sums[:, :subspace] * (1.0 / nverts)
    row = lax.broadcasted_iota(jnp.int32, (subspace, subspace), 0)
    column = lax.broadcasted_iota(jnp.int32, (subspace, subspace), 1)
    identity = (row == column).astype(jnp.float32)
    work, scale = eliminate(jnp.concatenate([gram, identity], 1), subspace, 8)
    solved = (work * scale)[:, subspace:]
    inverse[...] = solved
    basis[...] = jnp.dot(
        solved, filtered[...], precision=lax.Precision.HIGHEST, preferred_element_type=jnp.float32
    )


def project_kernel(nverts, sums, inverse, projected):
    subspace = inverse.shape[0]
    moment = sums[:, subspace:] * (0.5 / nverts)
    half = jnp.dot(
        inverse[...],
        moment + moment.T,
        precision=lax.Precision.HIGHEST,
        preferred_element_type=jnp.float32,
    )
    projected[...] = dot_rows(half, inverse[...], lax.Precision.HIGHEST)


def body(n_row, n_col, start_basis, degrees, tiles, tile_rows, tile_cols, counts):
    subspace, width = start_basis.shape
    slots_held, edge = tiles.shape[0], tiles.shape[1]
    per_part = width // edge
    nverts = n_row * n_col * width
    degrees = degrees[None, :]

    def swap(value, axis, size, distance):
        return lax.ppermute(value, axis, [(i, i ^ distance) for i in range(size)])

    def gather_row(value, behind=None):
        parts = [None] * n_row
        parts[0] = value
        for distance in range(2, n_row, 2):
            parts[distance] = swap(value, "row", n_row, distance)
        if behind is not None:
            parts[2::2], behind = lax.optimization_barrier((parts[2::2], behind))
        for distance in range(0, n_row, 2):
            parts[distance + 1] = swap(parts[distance], "row", n_row, 1)
        return parts if behind is None else (parts, behind)

    def gather_col(value):
        return [swap(value, "col", n_col, distance) for distance in range(1, n_col)]

    def vmem(count):
        return [pl.BlockSpec(memory_space=pltpu.VMEM)] * count

    scratch = [
        pltpu.VMEM((n_row * per_part, 2 * subspace, edge), jnp.bfloat16),
        pltpu.VMEM((n_col * per_part + 1, subspace, edge), jnp.float32),
    ]
    params = pltpu.CompilerParams(vmem_limit_bytes=20 * MIB)
    piece = jax.ShapeDtypeStruct((subspace, width), jnp.float32)
    high, low = pl.pallas_call(
        stage_kernel,
        out_shape=[jax.ShapeDtypeStruct(tiles.shape, jnp.bfloat16)] * 2,
        in_specs=[pl.BlockSpec(memory_space=pltpu.HBM)],
        out_specs=vmem(2),
        scratch_shapes=[
            pltpu.VMEM(tiles.shape, jnp.float32),
            pltpu.SemaphoreType.DMA((slots_held // 2,)),
        ],
        compiler_params=pltpu.CompilerParams(vmem_limit_bytes=42 * MIB),
        name="stage",
    )(tiles)

    parts, (high, low) = gather_row(start_basis, (high, low))
    parts[2], counts = lax.optimization_barrier((parts[2], counts))
    slots = pl.pallas_call(
        functools.partial(place_kernel, n_col, per_part),
        out_shape=jax.ShapeDtypeStruct((2, slots_held), jnp.int32),
        in_specs=vmem(3),
        out_specs=pl.BlockSpec(memory_space=pltpu.VMEM),
        compiler_params=params,
        name="places",
    )(tile_rows, tile_cols, counts)

    def products(parts):
        return pl.pallas_call(
            functools.partial(product_kernel, n_row, n_col),
            out_shape=[piece] * n_col,
            in_specs=vmem(3 + n_row),
            out_specs=vmem(n_col),
            scratch_shapes=scratch,
            compiler_params=params,
            name="tile_products",
        )(slots, high, low, *parts)

    def weights(parts):
        partial_values = products(parts)
        total = partial_values[0]
        for distance in reversed(range(1, n_col)):
            total = total + swap(partial_values[distance], "col", n_col, distance)
        return total

    def shifted(vectors, parts=None):
        parts = gather_row(vectors) if parts is None else parts
        return ((degrees - center_shift) * vectors - weights(parts)) / spread_radius

    previous = start_basis
    filtered = shifted(start_basis, parts)
    for level in range(DEGREE - 1):
        following = 2.0 * shifted(filtered) - previous
        previous, filtered = (filtered, following)

    parts = gather_row(filtered)
    beside = filtered
    sides = gather_col(beside)
    sides, parts[n_row // 2 + 1] = lax.optimization_barrier((sides, parts[n_row // 2 + 1]))
    pieces = products(parts)
    sums = pl.pallas_call(
        functools.partial(moment_kernel, n_row, n_col),
        out_shape=jax.ShapeDtypeStruct((subspace, 2 * subspace), jnp.float32),
        in_specs=vmem(n_row + 2 * n_col),
        out_specs=pl.BlockSpec(memory_space=pltpu.VMEM),
        compiler_params=params,
        name="moment",
    )(degrees, *parts, *sides, *pieces)
    sums = sum([swap(sums, "col", n_col, distance) for distance in range(1, n_col)], sums)
    inverse, basis = pl.pallas_call(
        functools.partial(factor_kernel, nverts),
        out_shape=[jax.ShapeDtypeStruct((subspace, subspace), jnp.float32), piece],
        in_specs=vmem(2),
        out_specs=vmem(2),
        compiler_params=params,
        name="factor",
    )(sums, filtered)
    arrived = [swap(sums, "row", n_row, distance) for distance in range(2, n_row, 2)]
    arrived, inverse = lax.optimization_barrier((arrived, inverse))
    sums = sum(arrived, sums)
    sums = sums + swap(sums, "row", n_row, 1)
    projected = pl.pallas_call(
        functools.partial(project_kernel, nverts),
        out_shape=jax.ShapeDtypeStruct((subspace, subspace), jnp.float32),
        in_specs=vmem(2),
        out_specs=pl.BlockSpec(memory_space=pltpu.VMEM),
        compiler_params=params,
        name="project",
    )(sums, inverse)
    return (basis, projected)


def solution(mesh):
    return jax.shard_map(
        functools.partial(body, mesh.shape["row"], mesh.shape["col"]),
        mesh=mesh,
        in_specs=(
            P(None, ("row", "col")),
            P(("row", "col")),
            P(("row", "col"), None, None),
            P("row", "col"),
            P("row", "col"),
            P("row", "col"),
        ),
        out_specs=(P(None, ("row", "col")), P()),
        check_vma=False,
    )
```

```python
import functools

import jax
import jax.numpy as jnp
from jax import lax
from jax.experimental import pallas as pl
from jax.experimental.pallas import tpu as pltpu
from jax.sharding import PartitionSpec as P

DEGREE = 3


center_shift = 1.0
spread_radius = 1.4
MIB = 1 << 20

ROWS_BY_ROWS = (((1,), (1,)), ((), ()))


def dot_rows(left, right, precision=None):
    return lax.dot_general(
        left, right, ROWS_BY_ROWS, precision=precision, preferred_element_type=jnp.float32
    )


def split(value):
    high = value.astype(jnp.bfloat16)
    low = (value - high.astype(jnp.float32)).astype(jnp.bfloat16)
    return high, low


def place_slots(n_col, per_part, rows, columns, counts):
    shift = per_part.bit_length() - 1
    row = rows[...] ^ (lax.axis_index("col") << shift)
    column = columns[...] ^ (lax.axis_index("row") << shift)
    live = lax.broadcasted_iota(jnp.int32, row.shape, 1) < counts[...]
    return jnp.concatenate([jnp.where(live, row, n_col * per_part), column], 0)


def place_kernel(n_col, per_part, rows, columns, counts, places):
    places[...] = place_slots(n_col, per_part, rows, columns, counts)


def stage_kernel(tiles, high, low, arrived, sems):
    chunks = sems.shape[0]
    width = tiles.shape[0] // chunks
    copies = [
        pltpu.make_async_copy(
            tiles.at[pl.ds(chunk * width, width)], arrived.at[pl.ds(chunk * width, width)], sems.at[chunk]
        )
        for chunk in range(chunks)
    ]
    for copy in copies:
        copy.start()
    for chunk, copy in enumerate(copies):
        copy.wait()
        for slot in range(chunk * width, (chunk + 1) * width):
            high[slot], low[slot] = split(arrived[slot].T)


def accumulate_tiles(slots, high, low, parts, halves, total):
    subspace = parts[0].shape[0]
    edge = high.shape[1]
    per_part = parts[0].shape[1] // edge
    places = slots[...]
    for index, part in enumerate(parts):
        for block in range(per_part):
            upper, lower = split(part[:, block * edge : (block + 1) * edge])
            halves[index * per_part + block, :subspace] = upper
            halves[index * per_part + block, subspace:] = lower
    total[...] = jnp.zeros_like(total)
    for slot in range(high.shape[0]):
        vectors = halves[places[1, slot]]
        first = jnp.dot(vectors, high[slot], preferred_element_type=jnp.float32)
        second = jnp.dot(vectors[:subspace], low[slot], preferred_element_type=jnp.float32)
        total[places[0, slot]] += first[:subspace] + first[subspace:] + second


def product_kernel(n_row, n_col, slots, high, low, *refs):
    parts, outs = refs[:n_row], refs[n_row : n_row + n_col]
    halves, total = refs[n_row + n_col :]
    accumulate_tiles(slots, high, low, parts, halves, total)
    edge = high.shape[1]
    per_part = parts[0].shape[1] // edge
    for index, out in enumerate(outs):
        for block in range(per_part):
            out[:, block * edge : (block + 1) * edge] = total[index * per_part + block]


def moment_kernel(n_row, n_col, degrees, *refs):
    parts, sides, products = refs[:n_row], refs[n_row : n_row + n_col - 1], refs[n_row + n_col - 1 : -1]
    out = refs[-1]
    subspace = parts[0].shape[0]

    def quarters(left, right):
        both = dot_rows(left, right)
        both = both[:subspace] + both[subspace:]
        return both[:, :subspace] + both[:, subspace:]

    own = parts[0][...]
    moment = dot_rows(own, own * degrees[...], lax.Precision.HIGHEST)
    gram = jnp.zeros_like(moment)
    for part in parts:
        both = jnp.concatenate(split(part[...]), 0)
        gram += quarters(both, both)
    for side, product in zip((parts[0], *sides), products):
        moment -= quarters(
            jnp.concatenate(split(side[...]), 0), jnp.concatenate(split(product[...]), 0)
        )
    out[...] = jnp.concatenate([gram, moment], 1)


def eliminate(work, size, panel):
    row = lax.broadcasted_iota(jnp.int32, work.shape, 0)
    pivots = jnp.ones_like(work)
    for first in range(0, size, panel):
        columns = [
            jnp.broadcast_to(work[:, index : index + 1], work.shape)
            for index in range(first, first + panel)
        ]
        for index in range(panel):
            step = first + index
            pivot = columns[index][step : step + 1, :]
            pivots = jnp.where(row == step, pivot, pivots)
            ratio = jnp.where(row > step, columns[index], 0.0) * (1.0 / pivot)
            work = work - ratio * work[step : step + 1, :]
            for later in range(index + 1, panel):
                columns[later] = columns[later] - ratio * columns[later][step : step + 1, :]
    return work, lax.rsqrt(pivots)


def factor_kernel(nverts, sums, filtered, inverse, basis):
    subspace = filtered.shape[0]
    gram = sums[:, :subspace] * (1.0 / nverts)
    row = lax.broadcasted_iota(jnp.int32, (subspace, subspace), 0)
    column = lax.broadcasted_iota(jnp.int32, (subspace, subspace), 1)
    identity = (row == column).astype(jnp.float32)
    work, scale = eliminate(jnp.concatenate([gram, identity], 1), subspace, 8)
    solved = (work * scale)[:, subspace:]
    inverse[...] = solved
    basis[...] = jnp.dot(
        solved, filtered[...], precision=lax.Precision.HIGHEST, preferred_element_type=jnp.float32
    )


def project_kernel(nverts, sums, inverse, projected):
    subspace = inverse.shape[0]
    moment = sums[:, subspace:] * (0.5 / nverts)
    half = jnp.dot(
        inverse[...],
        moment + moment.T,
        precision=lax.Precision.HIGHEST,
        preferred_element_type=jnp.float32,
    )
    projected[...] = dot_rows(half, inverse[...], lax.Precision.HIGHEST)


def body(n_row, n_col, start_basis, degrees, tiles, tile_rows, tile_cols, counts):
    subspace, width = start_basis.shape
    slots_held, edge = tiles.shape[0], tiles.shape[1]
    per_part = width // edge
    nverts = n_row * n_col * width
    degrees = degrees[None, :]

    def swap(value, axis, size, distance):
        return lax.ppermute(value, axis, [(i, i ^ distance) for i in range(size)])

    def gather_row(value, behind=None):
        parts = [None] * n_row
        parts[0] = value
        for distance in range(2, n_row, 2):
            parts[distance] = swap(value, "row", n_row, distance)
        if behind is not None:
            parts[2::2], behind = lax.optimization_barrier((parts[2::2], behind))
        for distance in range(0, n_row, 2):
            parts[distance + 1] = swap(parts[distance], "row", n_row, 1)
        return parts if behind is None else (parts, behind)

    def gather_col(value):
        held, distance = [value], 1
        while distance < n_col:
            held = held + [swap(part, "col", n_col, distance) for part in held]
            distance *= 2
        return held[1:]

    def vmem(count):
        return [pl.BlockSpec(memory_space=pltpu.VMEM)] * count

    scratch = [
        pltpu.VMEM((n_row * per_part, 2 * subspace, edge), jnp.bfloat16),
        pltpu.VMEM((n_col * per_part + 1, subspace, edge), jnp.float32),
    ]
    params = pltpu.CompilerParams(vmem_limit_bytes=20 * MIB)
    piece = jax.ShapeDtypeStruct((subspace, width), jnp.float32)
    high, low = pl.pallas_call(
        stage_kernel,
        out_shape=[jax.ShapeDtypeStruct(tiles.shape, jnp.bfloat16)] * 2,
        in_specs=[pl.BlockSpec(memory_space=pltpu.HBM)],
        out_specs=vmem(2),
        scratch_shapes=[
            pltpu.VMEM(tiles.shape, jnp.float32),
            pltpu.SemaphoreType.DMA((slots_held // 2,)),
        ],
        compiler_params=pltpu.CompilerParams(vmem_limit_bytes=42 * MIB),
        name="stage",
    )(tiles)

    parts, (high, low) = gather_row(start_basis, (high, low))
    parts[2], counts = lax.optimization_barrier((parts[2], counts))
    slots = pl.pallas_call(
        functools.partial(place_kernel, n_col, per_part),
        out_shape=jax.ShapeDtypeStruct((2, slots_held), jnp.int32),
        in_specs=vmem(3),
        out_specs=pl.BlockSpec(memory_space=pltpu.VMEM),
        compiler_params=params,
        name="places",
    )(tile_rows, tile_cols, counts)

    def products(parts):
        return pl.pallas_call(
            functools.partial(product_kernel, n_row, n_col),
            out_shape=[piece] * n_col,
            in_specs=vmem(3 + n_row),
            out_specs=vmem(n_col),
            scratch_shapes=scratch,
            compiler_params=params,
            name="tile_products",
        )(slots, high, low, *parts)

    def weights(parts):
        partial_values = products(parts)
        total = partial_values[0]
        for distance in reversed(range(1, n_col)):
            total = total + swap(partial_values[distance], "col", n_col, distance)
        return total

    def shifted(vectors, parts=None):
        parts = gather_row(vectors) if parts is None else parts
        return ((degrees - center_shift) * vectors - weights(parts)) / spread_radius

    previous = start_basis
    filtered = shifted(start_basis, parts)
    for level in range(DEGREE - 1):
        following = 2.0 * shifted(filtered) - previous
        previous, filtered = (filtered, following)

    parts = gather_row(filtered)
    beside = filtered
    sides = gather_col(beside)
    sides, parts[n_row // 2 + 1] = lax.optimization_barrier((sides, parts[n_row // 2 + 1]))
    pieces = products(parts)
    sums = pl.pallas_call(
        functools.partial(moment_kernel, n_row, n_col),
        out_shape=jax.ShapeDtypeStruct((subspace, 2 * subspace), jnp.float32),
        in_specs=vmem(n_row + 2 * n_col),
        out_specs=pl.BlockSpec(memory_space=pltpu.VMEM),
        compiler_params=params,
        name="moment",
    )(degrees, *parts, *sides, *pieces)
    sums = sum([swap(sums, "col", n_col, distance) for distance in range(1, n_col)], sums)
    inverse, basis = pl.pallas_call(
        functools.partial(factor_kernel, nverts),
        out_shape=[jax.ShapeDtypeStruct((subspace, subspace), jnp.float32), piece],
        in_specs=vmem(2),
        out_specs=vmem(2),
        compiler_params=params,
        name="factor",
    )(sums, filtered)
    arrived = [swap(sums, "row", n_row, distance) for distance in range(2, n_row, 2)]
    arrived, inverse = lax.optimization_barrier((arrived, inverse))
    sums = sum(arrived, sums)
    sums = sums + swap(sums, "row", n_row, 1)
    projected = pl.pallas_call(
        functools.partial(project_kernel, nverts),
        out_shape=jax.ShapeDtypeStruct((subspace, subspace), jnp.float32),
        in_specs=vmem(2),
        out_specs=pl.BlockSpec(memory_space=pltpu.VMEM),
        compiler_params=params,
        name="project",
    )(sums, inverse)
    return (basis, projected)


def solution(mesh):
    return jax.shard_map(
        functools.partial(body, mesh.shape["row"], mesh.shape["col"]),
        mesh=mesh,
        in_specs=(
            P(None, ("row", "col")),
            P(("row", "col")),
            P(("row", "col"), None, None),
            P("row", "col"),
            P("row", "col"),
            P("row", "col"),
        ),
        out_specs=(P(None, ("row", "col")), P()),
        check_vma=False,
    )
```

```python
import functools

import jax
import jax.numpy as jnp
from jax import lax
from jax.experimental import pallas as pl
from jax.experimental.pallas import tpu as pltpu
from jax.sharding import PartitionSpec as P

DEGREE = 3


center_shift = 1.0
spread_radius = 1.4
MIB = 1 << 20

ROWS_BY_ROWS = (((1,), (1,)), ((), ()))


def dot_rows(left, right, precision=None):
    return lax.dot_general(
        left, right, ROWS_BY_ROWS, precision=precision, preferred_element_type=jnp.float32
    )


def split(value):
    high = value.astype(jnp.bfloat16)
    low = (value - high.astype(jnp.float32)).astype(jnp.bfloat16)
    return high, low


def place_slots(n_col, per_part, rows, columns, counts):
    shift = per_part.bit_length() - 1
    row = rows[...] ^ (lax.axis_index("col") << shift)
    column = columns[...] ^ (lax.axis_index("row") << shift)
    live = lax.broadcasted_iota(jnp.int32, row.shape, 1) < counts[...]
    return jnp.concatenate([jnp.where(live, row, n_col * per_part), column], 0)


def place_kernel(n_col, per_part, rows, columns, counts, places):
    places[...] = place_slots(n_col, per_part, rows, columns, counts)


def stage_kernel(tiles, high, low, arrived, sems):
    chunks = sems.shape[0]
    width = tiles.shape[0] // chunks
    copies = [
        pltpu.make_async_copy(
            tiles.at[pl.ds(chunk * width, width)], arrived.at[pl.ds(chunk * width, width)], sems.at[chunk]
        )
        for chunk in range(chunks)
    ]
    for copy in copies:
        copy.start()
    for chunk, copy in enumerate(copies):
        copy.wait()
        for slot in range(chunk * width, (chunk + 1) * width):
            upper, lower = split(arrived[slot])
            high[slot], low[slot] = upper.T, lower.T


def accumulate_tiles(slots, high, low, parts, halves, total):
    subspace = parts[0].shape[0]
    edge = high.shape[1]
    per_part = parts[0].shape[1] // edge
    places = slots[...]
    for index, part in enumerate(parts):
        for block in range(per_part):
            upper, lower = split(part[:, block * edge : (block + 1) * edge])
            halves[index * per_part + block, :subspace] = upper
            halves[index * per_part + block, subspace:] = lower
    total[...] = jnp.zeros_like(total)
    for slot in range(high.shape[0]):
        vectors = halves[places[1, slot]]
        first = jnp.dot(vectors, high[slot], preferred_element_type=jnp.float32)
        second = jnp.dot(vectors[:subspace], low[slot], preferred_element_type=jnp.float32)
        total[places[0, slot]] += first[:subspace] + first[subspace:] + second


def product_kernel(n_row, n_col, slots, high, low, *refs):
    parts, outs = refs[:n_row], refs[n_row : n_row + n_col]
    halves, total = refs[n_row + n_col :]
    accumulate_tiles(slots, high, low, parts, halves, total)
    edge = high.shape[1]
    per_part = parts[0].shape[1] // edge
    for index, out in enumerate(outs):
        for block in range(per_part):
            out[:, block * edge : (block + 1) * edge] = total[index * per_part + block]


def moment_kernel(n_row, n_col, degrees, *refs):
    parts, sides, products = refs[:n_row], refs[n_row : n_row + n_col - 1], refs[n_row + n_col - 1 : -1]
    out = refs[-1]
    subspace = parts[0].shape[0]

    def quarters(left, right):
        both = dot_rows(left, right)
        both = both[:subspace] + both[subspace:]
        return both[:, :subspace] + both[:, subspace:]

    own = parts[0][...]
    moment = dot_rows(own, own * degrees[...], lax.Precision.HIGHEST)
    gram = jnp.zeros_like(moment)
    for part in parts:
        both = jnp.concatenate(split(part[...]), 0)
        gram += quarters(both, both)
    for side, product in zip((parts[0], *sides), products):
        moment -= quarters(
            jnp.concatenate(split(side[...]), 0), jnp.concatenate(split(product[...]), 0)
        )
    out[...] = jnp.concatenate([gram, moment], 1)


def eliminate(work, size, panel):
    row = lax.broadcasted_iota(jnp.int32, work.shape, 0)
    pivots = jnp.ones_like(work)
    for first in range(0, size, panel):
        columns = [
            jnp.broadcast_to(work[:, index : index + 1], work.shape)
            for index in range(first, first + panel)
        ]
        for index in range(panel):
            step = first + index
            pivot = columns[index][step : step + 1, :]
            pivots = jnp.where(row == step, pivot, pivots)
            ratio = jnp.where(row > step, columns[index], 0.0) * (1.0 / pivot)
            work = work - ratio * work[step : step + 1, :]
            for later in range(index + 1, panel):
                columns[later] = columns[later] - ratio * columns[later][step : step + 1, :]
    return work, lax.rsqrt(pivots)


def factor_kernel(nverts, sums, filtered, inverse, basis):
    subspace = filtered.shape[0]
    gram = sums[:, :subspace] * (1.0 / nverts)
    row = lax.broadcasted_iota(jnp.int32, (subspace, subspace), 0)
    column = lax.broadcasted_iota(jnp.int32, (subspace, subspace), 1)
    identity = (row == column).astype(jnp.float32)
    work, scale = eliminate(jnp.concatenate([gram, identity], 1), subspace, 8)
    solved = (work * scale)[:, subspace:]
    inverse[...] = solved
    basis[...] = jnp.dot(
        solved, filtered[...], precision=lax.Precision.HIGHEST, preferred_element_type=jnp.float32
    )


def project_kernel(nverts, sums, inverse, projected):
    subspace = inverse.shape[0]
    moment = sums[:, subspace:] * (0.5 / nverts)
    half = jnp.dot(
        inverse[...],
        moment + moment.T,
        precision=lax.Precision.HIGHEST,
        preferred_element_type=jnp.float32,
    )
    projected[...] = dot_rows(half, inverse[...], lax.Precision.HIGHEST)


def body(n_row, n_col, start_basis, degrees, tiles, tile_rows, tile_cols, counts):
    subspace, width = start_basis.shape
    slots_held, edge = tiles.shape[0], tiles.shape[1]
    per_part = width // edge
    nverts = n_row * n_col * width
    degrees = degrees[None, :]

    def swap(value, axis, size, distance):
        return lax.ppermute(value, axis, [(i, i ^ distance) for i in range(size)])

    def gather_row(value, behind=None):
        parts = [None] * n_row
        parts[0] = value
        for distance in range(2, n_row, 2):
            parts[distance] = swap(value, "row", n_row, distance)
        if behind is not None:
            parts[2::2], behind = lax.optimization_barrier((parts[2::2], behind))
        for distance in range(0, n_row, 2):
            parts[distance + 1] = swap(parts[distance], "row", n_row, 1)
        return parts if behind is None else (parts, behind)

    def gather_col(value):
        held, distance = [value], 1
        while distance < n_col:
            held = held + [swap(part, "col", n_col, distance) for part in held]
            distance *= 2
        return held[1:]

    def vmem(count):
        return [pl.BlockSpec(memory_space=pltpu.VMEM)] * count

    scratch = [
        pltpu.VMEM((n_row * per_part, 2 * subspace, edge), jnp.bfloat16),
        pltpu.VMEM((n_col * per_part + 1, subspace, edge), jnp.float32),
    ]
    params = pltpu.CompilerParams(vmem_limit_bytes=20 * MIB)
    piece = jax.ShapeDtypeStruct((subspace, width), jnp.float32)
    high, low = pl.pallas_call(
        stage_kernel,
        out_shape=[jax.ShapeDtypeStruct(tiles.shape, jnp.bfloat16)] * 2,
        in_specs=[pl.BlockSpec(memory_space=pltpu.HBM)],
        out_specs=vmem(2),
        scratch_shapes=[
            pltpu.VMEM(tiles.shape, jnp.float32),
            pltpu.SemaphoreType.DMA((slots_held // 8,)),
        ],
        compiler_params=pltpu.CompilerParams(vmem_limit_bytes=42 * MIB),
        name="stage",
    )(tiles)

    parts, (high, low) = gather_row(start_basis, (high, low))
    parts[2], counts = lax.optimization_barrier((parts[2], counts))
    slots = pl.pallas_call(
        functools.partial(place_kernel, n_col, per_part),
        out_shape=jax.ShapeDtypeStruct((2, slots_held), jnp.int32),
        in_specs=vmem(3),
        out_specs=pl.BlockSpec(memory_space=pltpu.VMEM),
        compiler_params=params,
        name="places",
    )(tile_rows, tile_cols, counts)

    def products(parts):
        return pl.pallas_call(
            functools.partial(product_kernel, n_row, n_col),
            out_shape=[piece] * n_col,
            in_specs=vmem(3 + n_row),
            out_specs=vmem(n_col),
            scratch_shapes=scratch,
            compiler_params=params,
            name="tile_products",
        )(slots, high, low, *parts)

    def weights(parts):
        partial_values = products(parts)
        total = partial_values[0]
        for distance in reversed(range(1, n_col)):
            total = total + swap(partial_values[distance], "col", n_col, distance)
        return total

    def shifted(vectors, parts=None):
        parts = gather_row(vectors) if parts is None else parts
        return ((degrees - center_shift) * vectors - weights(parts)) / spread_radius

    previous = start_basis
    filtered = shifted(start_basis, parts)
    for level in range(DEGREE - 1):
        following = 2.0 * shifted(filtered) - previous
        previous, filtered = (filtered, following)

    parts = gather_row(filtered)
    beside = filtered
    sides = gather_col(beside)
    sides, parts[n_row // 2 + 1] = lax.optimization_barrier((sides, parts[n_row // 2 + 1]))
    pieces = products(parts)
    sums = pl.pallas_call(
        functools.partial(moment_kernel, n_row, n_col),
        out_shape=jax.ShapeDtypeStruct((subspace, 2 * subspace), jnp.float32),
        in_specs=vmem(n_row + 2 * n_col),
        out_specs=pl.BlockSpec(memory_space=pltpu.VMEM),
        compiler_params=params,
        name="moment",
    )(degrees, *parts, *sides, *pieces)
    sums = sum([swap(sums, "col", n_col, distance) for distance in range(1, n_col)], sums)
    inverse, basis = pl.pallas_call(
        functools.partial(factor_kernel, nverts),
        out_shape=[jax.ShapeDtypeStruct((subspace, subspace), jnp.float32), piece],
        in_specs=vmem(2),
        out_specs=vmem(2),
        compiler_params=params,
        name="factor",
    )(sums, filtered)
    arrived = [swap(sums, "row", n_row, distance) for distance in range(2, n_row, 2)]
    arrived, inverse = lax.optimization_barrier((arrived, inverse))
    sums = sum(arrived, sums)
    sums = sums + swap(sums, "row", n_row, 1)
    projected = pl.pallas_call(
        functools.partial(project_kernel, nverts),
        out_shape=jax.ShapeDtypeStruct((subspace, subspace), jnp.float32),
        in_specs=vmem(2),
        out_specs=pl.BlockSpec(memory_space=pltpu.VMEM),
        compiler_params=params,
        name="project",
    )(sums, inverse)
    return (basis, projected)


def solution(mesh):
    return jax.shard_map(
        functools.partial(body, mesh.shape["row"], mesh.shape["col"]),
        mesh=mesh,
        in_specs=(
            P(None, ("row", "col")),
            P(("row", "col")),
            P(("row", "col"), None, None),
            P("row", "col"),
            P("row", "col"),
            P("row", "col"),
        ),
        out_specs=(P(None, ("row", "col")), P()),
        check_vma=False,
    )
```

```python
import functools

import jax
import jax.numpy as jnp
from jax import lax
from jax.experimental import pallas as pl
from jax.experimental.pallas import tpu as pltpu
from jax.sharding import PartitionSpec as P

DEGREE = 3


center_shift = 1.0
spread_radius = 1.4
MIB = 1 << 20

ROWS_BY_ROWS = (((1,), (1,)), ((), ()))


def dot_rows(left, right, precision=None):
    return lax.dot_general(
        left, right, ROWS_BY_ROWS, precision=precision, preferred_element_type=jnp.float32
    )


def split(value):
    high = value.astype(jnp.bfloat16)
    low = (value - high.astype(jnp.float32)).astype(jnp.bfloat16)
    return high, low


def place_slots(n_col, per_part, rows, columns, counts):
    shift = per_part.bit_length() - 1
    row = rows[...] ^ (lax.axis_index("col") << shift)
    column = columns[...] ^ (lax.axis_index("row") << shift)
    live = lax.broadcasted_iota(jnp.int32, row.shape, 1) < counts[...]
    return jnp.concatenate([jnp.where(live, row, n_col * per_part), column], 0)


def place_kernel(n_col, per_part, rows, columns, counts, places):
    places[...] = place_slots(n_col, per_part, rows, columns, counts)


def stage_kernel(tiles, high, low, arrived, sems):
    chunks = sems.shape[0]
    width = tiles.shape[0] // chunks
    copies = [
        pltpu.make_async_copy(
            tiles.at[pl.ds(chunk * width, width)], arrived.at[pl.ds(chunk * width, width)], sems.at[chunk]
        )
        for chunk in range(chunks)
    ]
    for copy in copies:
        copy.start()
    for chunk, copy in enumerate(copies):
        copy.wait()
        for slot in range(chunk * width, (chunk + 1) * width):
            upper, lower = split(arrived[slot])
            high[slot], low[slot] = upper.T, lower.T


def accumulate_tiles(slots, high, low, parts, halves, total):
    subspace = parts[0].shape[0]
    edge = high.shape[1]
    per_part = parts[0].shape[1] // edge
    places = slots[...]
    for index, part in enumerate(parts):
        for block in range(per_part):
            upper, lower = split(part[:, block * edge : (block + 1) * edge])
            halves[index * per_part + block, :subspace] = upper
            halves[index * per_part + block, subspace:] = lower
    total[...] = jnp.zeros_like(total)
    for slot in range(high.shape[0]):
        vectors = halves[places[1, slot]]
        first = jnp.dot(vectors, high[slot], preferred_element_type=jnp.float32)
        second = jnp.dot(vectors[:subspace], low[slot], preferred_element_type=jnp.float32)
        total[places[0, slot]] += first[:subspace] + first[subspace:] + second


def product_kernel(n_row, n_col, slots, high, low, *refs):
    parts, outs = refs[:n_row], refs[n_row : n_row + n_col]
    halves, total = refs[n_row + n_col :]
    accumulate_tiles(slots, high, low, parts, halves, total)
    edge = high.shape[1]
    per_part = parts[0].shape[1] // edge
    for index, out in enumerate(outs):
        for block in range(per_part):
            out[:, block * edge : (block + 1) * edge] = total[index * per_part + block]


def moment_kernel(n_row, n_col, degrees, *refs):
    parts, sides, products = refs[:n_row], refs[n_row : n_row + n_col - 1], refs[n_row + n_col - 1 : -1]
    out = refs[-1]
    subspace = parts[0].shape[0]

    def quarters(left, right):
        both = dot_rows(left, right)
        both = both[:subspace] + both[subspace:]
        return both[:, :subspace] + both[:, subspace:]

    own = parts[0][...]
    moment = quarters(
        jnp.concatenate(split(own), 0), jnp.concatenate(split(own * degrees[...]), 0)
    )
    gram = jnp.zeros_like(moment)
    for part in parts:
        both = jnp.concatenate(split(part[...]), 0)
        gram += quarters(both, both)
    for side, product in zip((parts[0], *sides), products):
        moment -= quarters(
            jnp.concatenate(split(side[...]), 0), jnp.concatenate(split(product[...]), 0)
        )
    out[...] = jnp.concatenate([gram, moment], 1)


def eliminate(work, size, panel):
    row = lax.broadcasted_iota(jnp.int32, work.shape, 0)
    pivots = jnp.ones_like(work)
    for first in range(0, size, panel):
        columns = [
            jnp.broadcast_to(work[:, index : index + 1], work.shape)
            for index in range(first, first + panel)
        ]
        for index in range(panel):
            step = first + index
            pivot = columns[index][step : step + 1, :]
            pivots = jnp.where(row == step, pivot, pivots)
            ratio = jnp.where(row > step, columns[index], 0.0) * (1.0 / pivot)
            work = work - ratio * work[step : step + 1, :]
            for later in range(index + 1, panel):
                columns[later] = columns[later] - ratio * columns[later][step : step + 1, :]
    return work, lax.rsqrt(pivots)


def factor_kernel(nverts, sums, filtered, inverse, basis):
    subspace = filtered.shape[0]
    gram = sums[:, :subspace] * (1.0 / nverts)
    row = lax.broadcasted_iota(jnp.int32, (subspace, subspace), 0)
    column = lax.broadcasted_iota(jnp.int32, (subspace, subspace), 1)
    identity = (row == column).astype(jnp.float32)
    work, scale = eliminate(jnp.concatenate([gram, identity], 1), subspace, 8)
    solved = (work * scale)[:, subspace:]
    inverse[...] = solved
    basis[...] = jnp.dot(
        solved, filtered[...], precision=lax.Precision.HIGHEST, preferred_element_type=jnp.float32
    )


def project_kernel(nverts, sums, inverse, projected):
    subspace = inverse.shape[0]
    moment = sums[:, subspace:] * (0.5 / nverts)
    half = jnp.dot(
        inverse[...],
        moment + moment.T,
        precision=lax.Precision.HIGHEST,
        preferred_element_type=jnp.float32,
    )
    projected[...] = dot_rows(half, inverse[...], lax.Precision.HIGHEST)


def body(n_row, n_col, start_basis, degrees, tiles, tile_rows, tile_cols, counts):
    subspace, width = start_basis.shape
    slots_held, edge = tiles.shape[0], tiles.shape[1]
    per_part = width // edge
    nverts = n_row * n_col * width
    degrees = degrees[None, :]

    def swap(value, axis, size, distance):
        return lax.ppermute(value, axis, [(i, i ^ distance) for i in range(size)])

    def gather_row(value, behind=None):
        parts = [None] * n_row
        parts[0] = value
        for distance in range(2, n_row, 2):
            parts[distance] = swap(value, "row", n_row, distance)
        if behind is not None:
            parts[2::2], behind = lax.optimization_barrier((parts[2::2], behind))
        for distance in range(0, n_row, 2):
            parts[distance + 1] = swap(parts[distance], "row", n_row, 1)
        return parts if behind is None else (parts, behind)

    def gather_col(value):
        held, distance = [value], 1
        while distance < n_col:
            held = held + [swap(part, "col", n_col, distance) for part in held]
            distance *= 2
        return held[1:]

    def vmem(count):
        return [pl.BlockSpec(memory_space=pltpu.VMEM)] * count

    scratch = [
        pltpu.VMEM((n_row * per_part, 2 * subspace, edge), jnp.bfloat16),
        pltpu.VMEM((n_col * per_part + 1, subspace, edge), jnp.float32),
    ]
    params = pltpu.CompilerParams(vmem_limit_bytes=20 * MIB)
    piece = jax.ShapeDtypeStruct((subspace, width), jnp.float32)
    high, low = pl.pallas_call(
        stage_kernel,
        out_shape=[jax.ShapeDtypeStruct(tiles.shape, jnp.bfloat16)] * 2,
        in_specs=[pl.BlockSpec(memory_space=pltpu.HBM)],
        out_specs=vmem(2),
        scratch_shapes=[
            pltpu.VMEM(tiles.shape, jnp.float32),
            pltpu.SemaphoreType.DMA((slots_held // 8,)),
        ],
        compiler_params=pltpu.CompilerParams(vmem_limit_bytes=42 * MIB),
        name="stage",
    )(tiles)

    parts, (high, low) = gather_row(start_basis, (high, low))
    parts[2], counts = lax.optimization_barrier((parts[2], counts))
    slots = pl.pallas_call(
        functools.partial(place_kernel, n_col, per_part),
        out_shape=jax.ShapeDtypeStruct((2, slots_held), jnp.int32),
        in_specs=vmem(3),
        out_specs=pl.BlockSpec(memory_space=pltpu.VMEM),
        compiler_params=params,
        name="places",
    )(tile_rows, tile_cols, counts)

    def products(parts):
        return pl.pallas_call(
            functools.partial(product_kernel, n_row, n_col),
            out_shape=[piece] * n_col,
            in_specs=vmem(3 + n_row),
            out_specs=vmem(n_col),
            scratch_shapes=scratch,
            compiler_params=params,
            name="tile_products",
        )(slots, high, low, *parts)

    def weights(parts):
        partial_values = products(parts)
        total = partial_values[0]
        for distance in reversed(range(1, n_col)):
            total = total + swap(partial_values[distance], "col", n_col, distance)
        return total

    def shifted(vectors, parts=None):
        parts = gather_row(vectors) if parts is None else parts
        return ((degrees - center_shift) * vectors - weights(parts)) / spread_radius

    previous = start_basis
    filtered = shifted(start_basis, parts)
    for level in range(DEGREE - 1):
        following = 2.0 * shifted(filtered) - previous
        previous, filtered = (filtered, following)

    parts = gather_row(filtered)
    beside = filtered
    sides = gather_col(beside)
    sides, parts[n_row // 2 + 1] = lax.optimization_barrier((sides, parts[n_row // 2 + 1]))
    pieces = products(parts)
    sums = pl.pallas_call(
        functools.partial(moment_kernel, n_row, n_col),
        out_shape=jax.ShapeDtypeStruct((subspace, 2 * subspace), jnp.float32),
        in_specs=vmem(n_row + 2 * n_col),
        out_specs=pl.BlockSpec(memory_space=pltpu.VMEM),
        compiler_params=params,
        name="moment",
    )(degrees, *parts, *sides, *pieces)
    sums = sum([swap(sums, "col", n_col, distance) for distance in range(1, n_col)], sums)
    inverse, basis = pl.pallas_call(
        functools.partial(factor_kernel, nverts),
        out_shape=[jax.ShapeDtypeStruct((subspace, subspace), jnp.float32), piece],
        in_specs=vmem(2),
        out_specs=vmem(2),
        compiler_params=params,
        name="factor",
    )(sums, filtered)
    arrived = [swap(sums, "row", n_row, distance) for distance in range(2, n_row, 2)]
    arrived, inverse = lax.optimization_barrier((arrived, inverse))
    sums = sum(arrived, sums)
    sums = sums + swap(sums, "row", n_row, 1)
    projected = pl.pallas_call(
        functools.partial(project_kernel, nverts),
        out_shape=jax.ShapeDtypeStruct((subspace, subspace), jnp.float32),
        in_specs=vmem(2),
        out_specs=pl.BlockSpec(memory_space=pltpu.VMEM),
        compiler_params=params,
        name="project",
    )(sums, inverse)
    return (basis, projected)


def solution(mesh):
    return jax.shard_map(
        functools.partial(body, mesh.shape["row"], mesh.shape["col"]),
        mesh=mesh,
        in_specs=(
            P(None, ("row", "col")),
            P(("row", "col")),
            P(("row", "col"), None, None),
            P("row", "col"),
            P("row", "col"),
            P("row", "col"),
        ),
        out_specs=(P(None, ("row", "col")), P()),
        check_vma=False,
    )
```
